32 devices in a mesh: groups: 2 (over x), cx: 16 (over z, y, core).
Axes of the slice: x: 2, y: 2, z: 4, core: 2. Of those that a mesh axis runs over, the one named last changes fastest.
Arguments:
- displacements: bfloat16 [512, 3, 5120], P(('groups', 'cx')), parts along dimension 0, may hold values from -6 to 6
- forces: bfloat16 [512, 3, 5120], P(('groups', 'cx')), parts along dimension 0, may hold values from -6 to 6
- phi: bfloat16 [160, 14, 192, 192], P(('groups', 'cx')), parts along dimension 0, may hold values from -0.125 to 0.125
- neighbours: int32 [80, 14], P('cx'), may hold values from 0 to 79, as said below
- cluster_atoms: int32 [80, 64], P('cx'), may hold values from 0 to 5119, as said below
- config_order: int32 [512], P('groups'), parts along dimension 0, may hold values from 0 to 255, each once
- weights: float32 [512], P('groups'), parts along dimension 0, may hold values from 0.02 to 0.3
Outputs:
- residual: bfloat16 [160, 192, 256], P(('groups', 'cx')), parts along dimension 0
- gradient: bfloat16 [160, 14, 192, 192], P(('groups', 'cx')), parts along dimension 0
The draws below stay inside these ranges and needn't reach their ends.
There are 2 independent parts, one for each index of `groups`. The reference program is written for one: setup_inputs(seed, part) draws one part's arguments, and reference() takes and returns one part's arrays. A program takes and returns all parts, laid end to end along the dimension named above; an argument that names none is the same for every part. Nothing has to cross between parts.
Inputs may be any that keep to these rules, and one draw needn't show every extreme that they name: `neighbours`: cluster c lies in layer c // 5 of 16 periodic layers; its 14 blocks name distinct clusters of its own layer and the two layers beside it, wrapping at the ends. `cluster_atoms`: the clusters of layer j hold the atoms 5 * 64 * j to 5 * 64 * (j + 1) - 1, each once. `config_order`: each ensemble index once.
All inputs are finite; a program needn't handle non-finite values.
Results may differ from the reference program's by a relative error of at most 0.0085.
Values may be sent and summed in bfloat16 or wider, within the bound.
A program may use at most 128 MiB of HBM per device.

```python
import math
import jax
import jax.numpy as jnp
from jax import lax

CONFIGS = 256
ATOMS = 64
LAYER = 5
BLOCKS = 14
DOF = 192
CLUSTERS = 80
NATOM = 5120


def draw_neighbours(key, part):
    layers = CLUSTERS // LAYER
    keys = jax.random.split(jax.random.fold_in(key, 11), CLUSTERS)

    def pick_one(subkey):
        return jax.random.permutation(subkey, 3 * LAYER)[:BLOCKS]
    picks = jax.vmap(pick_one)(keys).astype(jnp.int32)
    layer_of = (jnp.arange(CLUSTERS, dtype=jnp.int32) // LAYER)[:, None]
    offset = picks // LAYER - 1
    within = picks % LAYER
    return ((layer_of + offset + layers) % layers * LAYER + within).astype(jnp.int32)


def draw_cluster_atoms(key, part):
    layers = CLUSTERS // LAYER
    keys = jax.random.split(jax.random.fold_in(key, 23), layers)

    def layer_atoms(subkey):
        return jax.random.permutation(subkey, LAYER * ATOMS).astype(jnp.int32)
    picks = jax.vmap(layer_atoms)(keys)
    starts = (jnp.arange(layers, dtype=jnp.int32) * (LAYER * ATOMS))[:, None]
    return (picks + starts).reshape(CLUSTERS, ATOMS).astype(jnp.int32)


def levels(stream_key, dims, cuts, smallest, high):
    gain = 1.0
    for axis_at, parts in cuts:
        heights = jax.random.uniform(jax.random.fold_in(jax.random.fold_in(stream_key, 6), axis_at), (parts,), jnp.float32, smallest / len(cuts), high / len(cuts))
        gain = gain * jnp.repeat(jnp.exp(heights), dims[axis_at] // parts).reshape((-1,) + (1,) * (len(dims) - 1 - axis_at))
    return gain


def noise(key, extent, scale, reach, shards=(), held_as=jnp.bfloat16):
    result = jax.random.normal(key, extent, jnp.float32) * scale
    if len(shards) > 0:
        result = levels(key, extent, shards, -0.22, 0.18) * result
    return jnp.clip(result, min=-reach, max=reach).astype(held_as)


def setup_inputs(seed: int = 0, part: int = 0) -> dict:
    key_list = jax.random.split(jax.random.key(seed), 8)
    own_keys = jax.random.split(jax.random.fold_in(key_list[7], part), 8)
    return {
        "displacements": noise(own_keys[0], (CONFIGS, 3, NATOM), 1.0, 6.0, ((0, 16),)),
        "forces": noise(own_keys[1], (CONFIGS, 3, NATOM), 1.0, 6.0, ((0, 16),)),
        "phi": noise(own_keys[2], (CLUSTERS, BLOCKS, DOF, DOF), (BLOCKS * DOF) ** -0.5, 0.125, ((0, 16),)),
        "neighbours": draw_neighbours(jax.random.fold_in(key_list[7], 71), part),
        "cluster_atoms": draw_cluster_atoms(jax.random.fold_in(key_list[7], 71), part),
        "config_order": jax.random.permutation(own_keys[5], CONFIGS).astype(jnp.int32),
        "weights": jnp.clip(jnp.exp(jax.random.uniform(own_keys[6], (CONFIGS,), jnp.float32, math.log(0.02), math.log(0.3))), 0.02, 0.3),
    }


def arrange(field, atom_map):
    picked = jnp.take(field, atom_map.reshape(-1), axis=2)
    picked = picked.reshape(field.shape[0], 3, atom_map.shape[0], atom_map.shape[1])
    return jnp.transpose(picked, (2, 1, 3, 0)).reshape(atom_map.shape[0], 3 * atom_map.shape[1], field.shape[0])


def reference(displacements, forces, phi, neighbours, cluster_atoms, config_order, weights):
    cdisp = arrange(displacements, cluster_atoms)
    cforce = arrange(forces, cluster_atoms)
    index_all = jnp.arange(CLUSTERS, dtype=jnp.int32)

    def harm_one(cluster):
        near = jnp.take(cdisp, neighbours[cluster], axis=0).astype(jnp.float32)
        return jnp.einsum('kij,kjs->is', phi[cluster].astype(jnp.float32), near)

    harmonic = lax.map(harm_one, index_all)
    residual = (cforce.astype(jnp.float32) + harmonic).astype(jnp.bfloat16)
    match = config_order[:, None] == jnp.arange(CONFIGS, dtype=jnp.int32)[None, :]
    weight_row = jnp.sum(jnp.where(match, weights[None, :], jnp.zeros_like(weights)[None, :]), axis=1)
    wres = (residual.astype(jnp.float32) * weight_row[None, None, :]).astype(jnp.bfloat16)
    wdisp = (cdisp.astype(jnp.float32) * weight_row[None, None, :]).astype(jnp.bfloat16)

    def grad_one(cluster):
        near_disp = jnp.take(cdisp, neighbours[cluster], axis=0).astype(jnp.float32)
        near_resid = jnp.take(residual, neighbours[cluster], axis=0).astype(jnp.float32)
        first = jnp.einsum('is,kjs->kij', wres[cluster].astype(jnp.float32), near_disp)
        second = jnp.einsum('is,kjs->kij', wdisp[cluster].astype(jnp.float32), near_resid)
        return (0.5 * (first + second)).astype(jnp.bfloat16)

    gradient = lax.map(grad_one, index_all)
    return (residual, gradient)
```

```python
import functools

import jax
import jax.numpy as jnp
from jax import lax
from jax.experimental import pallas as pl
from jax.experimental.pallas import tpu as pltpu
from jax.sharding import PartitionSpec as P

LANES = 128
SUBLANES = 16
ANY = pl.BlockSpec(memory_space=pl.ANY)
VMEM = pl.BlockSpec(memory_space=pltpu.VMEM)
SMEM = pl.BlockSpec(memory_space=pltpu.SMEM)
NT = (((1,), (1,)), ((), ()))


def column(row):
    m = row.shape[1]
    eye = lax.broadcasted_iota(jnp.int32, (m, m), 0) == lax.broadcasted_iota(
        jnp.int32, (m, m), 1
    )
    return jnp.sum(jnp.where(eye, row, jnp.zeros_like(row)), axis=1, keepdims=True)


def exchange(
    n, rows, span,
    disp, force, phi, near, atoms, order, weights,
    frame_disp, frame_resid, sides,
    phi_v, got_disp, got_force, pick, cdisp, cforce, resid, wt,
    own_sem, phi_sem, send_sem, recv_sem, halo_send, halo_recv, back_send, back_recv, out_sem,
):
    layer, size = atoms.shape
    blocks = phi.shape[1]
    padded, width = got_disp.shape[2:]
    me = lax.axis_index("cx")
    right, left = lax.rem(me + 1, n), lax.rem(me + n - 1, n)

    def start_of(owner):
        return pl.multiple_of((owner * span) // LANES * LANES, LANES)

    phi_copies = [
        pltpu.make_async_copy(phi.at[c], phi_v.at[c], phi_sem.at[c]) for c in range(layer)
    ]
    fields = ((disp, got_disp), (force, got_force))
    own_copies = [
        pltpu.make_async_copy(src.at[:, :, pl.ds(start_of(me), width)], dst.at[me], own_sem.at[i])
        for i, (src, dst) in enumerate(fields)
    ]

    barrier = pltpu.get_barrier_semaphore()

    @pl.loop(1, n)
    def _(i):
        pl.semaphore_signal(barrier, inc=1, device_id={"cx": lax.rem(me + i, n)})

    for copy in own_copies:
        copy.start()

    shift = me * span - (me * span) // LANES * LANES
    for c in range(layer):
        place = column((atoms[c : c + 1, :] - me * span + shift).astype(jnp.float32))
        lane = lax.broadcasted_iota(jnp.int32, (size, width), 1).astype(jnp.float32)
        pick[c * size : (c + 1) * size, :] = jnp.where(lane == place, 1.0, 0.0).astype(jnp.bfloat16)
    configs = order.shape[1]
    match = order[...] == lax.broadcasted_iota(jnp.int32, (configs, configs), 0)
    wt[...] = jnp.sum(jnp.where(match, column(weights[...]), 0.0), axis=0, keepdims=True)

    pl.semaphore_wait(barrier, n - 1)

    def moved(field, i, owner):
        src, dst = fields[field]
        peer = lax.rem(me + i, n)
        return pltpu.make_async_remote_copy(
            src_ref=src.at[:, :, pl.ds(start_of(peer), width)],
            dst_ref=dst.at[owner],
            send_sem=send_sem.at[field, i],
            recv_sem=recv_sem.at[field, i],
            device_id={"cx": peer},
        )

    for field in range(2):

        @pl.loop(1, n)
        def _(i):
            moved(field, i, me).start()

    for copy in phi_copies:
        copy.start()

    def gathered(field, store):
        own_copies[field].wait()

        @pl.loop(1, n)
        def _(i):
            moved(field, i, lax.rem(me + n - i, n)).wait_recv()

        for a in range(3):
            x = fields[field][1][:, a].reshape(n * padded, width)
            y = lax.dot_general(pick[...], x, NT, preferred_element_type=jnp.float32)
            if padded != rows:
                sub = lax.broadcasted_iota(jnp.int32, (n * padded, n * rows), 0)
                col = lax.broadcasted_iota(jnp.int32, (n * padded, n * rows), 1)
                keep = sub == col // rows * padded + col % rows
                y = jnp.dot(
                    y.astype(jnp.bfloat16),
                    jnp.where(keep, 1.0, 0.0).astype(jnp.bfloat16),
                    preferred_element_type=jnp.float32,
                )
            for c in range(layer):
                store(c, a, y[c * size : (c + 1) * size, :])

    def keep_disp(c, a, value):
        cdisp[layer + c, a * size : (a + 1) * size, :] = value.astype(jnp.bfloat16)

    def keep_force(c, a, value):
        cforce[c, a * size : (a + 1) * size, :] = value

    gathered(0, keep_disp)
    middle = pl.ds(layer, layer)
    halo = [
        pltpu.make_async_remote_copy(
            src_ref=cdisp.at[middle],
            dst_ref=cdisp.at[pl.ds(place, layer)],
            send_sem=halo_send.at[i],
            recv_sem=halo_recv.at[i],
            device_id={"cx": peer},
        )
        for i, (peer, place) in enumerate(((right, 0), (left, 2 * layer)))
    ]
    for copy in halo:
        copy.start()
    gathered(1, keep_force)
    for copy in halo:
        copy.wait_recv()
    disp_out = pltpu.make_async_copy(cdisp, frame_disp, out_sem.at[0])
    disp_out.start()
    for copy in phi_copies:
        copy.wait()

    def back(c, side):
        peer, place = ((right, 0), (left, 2 * layer))[side]
        return pltpu.make_async_remote_copy(
            src_ref=resid.at[c],
            dst_ref=frame_resid.at[place + c],
            send_sem=back_send.at[side, c],
            recv_sem=back_recv.at[side, c],
            device_id={"cx": peer},
        )

    def keep(c):
        return pltpu.make_async_copy(resid.at[c], frame_resid.at[layer + c], out_sem.at[1 + c])

    dof = 3 * size

    @pl.loop(0, layer)
    def _(c):
        total = cforce[c]
        for k in range(blocks):
            name = near[c, k]
            offset = jnp.minimum(lax.rem(name // layer - me + 1 + n, n), 2)
            total += jnp.dot(
                phi_v[c, k],
                cdisp[offset * layer + lax.rem(name, layer)],
                preferred_element_type=jnp.float32,
            )
        rounded = total.astype(jnp.bfloat16)
        resid[c] = rounded
        back(c, 0).start()
        back(c, 1).start()
        keep(c).start()
        sides[c, :, :configs] = (rounded.astype(jnp.float32) * wt[...]).astype(jnp.bfloat16)
        sides[c, :, configs:] = (cdisp[layer + c].astype(jnp.float32) * wt[...]).astype(
            jnp.bfloat16
        )

    for field in range(2):

        @pl.loop(1, n)
        def _(i):
            moved(field, i, me).wait_send()

    for copy in halo:
        copy.wait_send()
    disp_out.wait()
    for c in range(layer):
        keep(c).wait()
        for side in range(2):
            back(c, side).wait()


def products(n, layer, near, position, sides, disp, resid, residual, gradient):
    c = pl.program_id(0)
    blocks = gradient.shape[1]
    configs = disp.shape[2]
    me = position[0]
    residual[0] = resid[layer + c]
    for k in range(blocks):
        name = near[c, k]
        offset = jnp.minimum(lax.rem(name // layer - me + 1 + n, n), 2)
        index = offset * layer + lax.rem(name, layer)
        total = lax.dot_general(
            sides[0, :, :configs], disp[index], NT, preferred_element_type=jnp.float32
        ) + lax.dot_general(
            sides[0, :, configs:], resid[index], NT, preferred_element_type=jnp.float32
        )
        gradient[0, k] = (0.5 * total).astype(jnp.bfloat16)


def shards(n, displacements, forces, phi, neighbours, cluster_atoms, config_order, weights):
    rows, _, atoms = displacements.shape
    layer, size = cluster_atoms.shape
    blocks, dof = phi.shape[1:3]
    configs = config_order.shape[0]
    span = atoms // n
    width = -(-span // LANES) * LANES
    while any((p * span) % LANES + span > width for p in range(n)):
        width += LANES
    padded = -(-rows // SUBLANES) * SUBLANES

    def laid(field):
        field = jnp.transpose(field, (1, 0, 2))
        if padded != rows:
            field = jnp.pad(field, ((0, 0), (0, padded - rows), (0, 0)))
        return field

    bf16 = jnp.bfloat16
    dma = pltpu.SemaphoreType.DMA
    frame = jax.ShapeDtypeStruct((3 * layer, dof, configs), bf16)
    frame_disp, frame_resid, sides = pl.pallas_call(
        functools.partial(exchange, n, rows, span),
        out_shape=[frame, frame, jax.ShapeDtypeStruct((layer, dof, 2 * configs), bf16)],
        in_specs=[ANY, ANY, ANY, SMEM, VMEM, VMEM, VMEM],
        out_specs=[ANY, ANY, VMEM],
        scratch_shapes=[
            pltpu.VMEM(phi.shape, bf16),
            pltpu.VMEM((n, 3, padded, width), bf16),
            pltpu.VMEM((n, 3, padded, width), bf16),
            pltpu.VMEM((layer * size, width), bf16),
            pltpu.VMEM((3 * layer, dof, configs), bf16),
            pltpu.VMEM((layer, dof, configs), jnp.float32),
            pltpu.VMEM((layer, dof, configs), bf16),
            pltpu.VMEM((1, configs), jnp.float32),
            dma((2,)),
            dma((layer,)),
            dma((2, n)),
            dma((2, n)),
            dma((2,)),
            dma((2,)),
            dma((2, layer)),
            dma((2, layer)),
            dma((1 + layer,)),
        ],
        compiler_params=pltpu.CompilerParams(
            collective_id=0, has_side_effects=True, vmem_limit_bytes=32 * 1024 * 1024
        ),
    )(
        laid(displacements),
        laid(forces),
        phi,
        neighbours,
        cluster_atoms,
        config_order.reshape(1, configs),
        weights.reshape(1, configs),
    )
    position = lax.axis_index("cx").reshape(1).astype(jnp.int32)
    whole = pl.BlockSpec((3 * layer, dof, configs), lambda c: (0, 0, 0))
    return pl.pallas_call(
        functools.partial(products, n, layer),
        grid=(layer,),
        out_shape=[
            jax.ShapeDtypeStruct((layer, dof, configs), bf16),
            jax.ShapeDtypeStruct(phi.shape, bf16),
        ],
        in_specs=[
            SMEM,
            SMEM,
            pl.BlockSpec((1, dof, 2 * configs), lambda c: (c, 0, 0)),
            whole,
            whole,
        ],
        out_specs=[
            pl.BlockSpec((1, dof, configs), lambda c: (c, 0, 0)),
            pl.BlockSpec((1, blocks, dof, dof), lambda c: (c, 0, 0, 0)),
        ],
        compiler_params=pltpu.CompilerParams(vmem_limit_bytes=32 * 1024 * 1024),
    )(neighbours, position, sides, frame_disp, frame_resid)


def solution(mesh):
    in_specs = (
        P(("groups", "cx"), None, None),
        P(("groups", "cx"), None, None),
        P(("groups", "cx"), None, None, None),
        P("cx", None),
        P("cx", None),
        P("groups"),
        P("groups"),
    )
    out_specs = (P(("groups", "cx"), None, None), P(("groups", "cx"), None, None, None))
    return jax.shard_map(
        functools.partial(shards, mesh.shape["cx"]),
        mesh=mesh,
        in_specs=in_specs,
        out_specs=out_specs,
        check_vma=False,
    )
```

```python
import functools

import jax
import jax.numpy as jnp
from jax import lax
from jax.experimental import pallas as pl
from jax.experimental.pallas import tpu as pltpu
from jax.sharding import PartitionSpec as P

LANES = 128
SUBLANES = 16
ANY = pl.BlockSpec(memory_space=pl.ANY)
VMEM = pl.BlockSpec(memory_space=pltpu.VMEM)
SMEM = pl.BlockSpec(memory_space=pltpu.SMEM)
NT = (((1,), (1,)), ((), ()))


def column(row):
    m = row.shape[1]
    eye = lax.broadcasted_iota(jnp.int32, (m, m), 0) == lax.broadcasted_iota(
        jnp.int32, (m, m), 1
    )
    return jnp.sum(jnp.where(eye, row, jnp.zeros_like(row)), axis=1, keepdims=True)


def exchange(
    n, rows, span,
    disp, force, phi, near_in, atoms_in, order_in, weights_in,
    frame_disp, frame_resid, sides,
    near, atoms, order, weights,
    phi_v, raw_disp, raw_force, made_disp, made_force, got_disp, got_force, pick, cdisp, cforce, resid, wt, small_sem,
    raw_sem, own_sem, phi_sem, send_sem, recv_sem, halo_send, halo_recv, back_send, back_recv, out_sem,
):
    layer, size = atoms.shape
    blocks = phi.shape[1]
    slots, padded = got_disp.shape[1:3]
    full = (slots - 2) // 3
    edge = full * LANES
    half = LANES // 2
    me = lax.axis_index("cx")
    right, left = lax.rem(me + 1, n), lax.rem(me + n - 1, n)

    phi_copies = [
        pltpu.make_async_copy(phi.at[c], phi_v.at[c], phi_sem.at[c]) for c in range(layer)
    ]
    fields = ((raw_disp, made_disp, got_disp), (raw_force, made_force, got_force))
    raw_copies = [
        pltpu.make_async_copy(src, fields[i][0], raw_sem.at[i]) for i, src in enumerate((disp, force))
    ]
    own_copies = [
        pltpu.make_async_copy(made.at[me], got.at[me], own_sem.at[i])
        for i, (_, made, got) in enumerate(fields)
    ]
    small_copies = [
        pltpu.make_async_copy(src, dst, small_sem.at[i])
        for i, (src, dst) in enumerate(
            ((near_in, near), (atoms_in, atoms), (order_in, order), (weights_in, weights))
        )
    ]
    barrier = pltpu.get_barrier_semaphore()

    @pl.loop(1, n)
    def _(i):
        pl.semaphore_signal(barrier, inc=1, device_id={"cx": lax.rem(me + i, n)})

    for copy in raw_copies + small_copies:
        copy.start()

    lane = lax.broadcasted_iota(jnp.int32, (padded, LANES), 1)

    def pack(field):
        raw, made, _ = fields[field]

        @pl.loop(0, n // 2)
        def _(pair):
            base = pair * (2 * span)

            def tile(a, t):
                return raw[a, :, pl.ds(pl.multiple_of(base + t * LANES, LANES), LANES)]

            for a in range(3):
                for t in range(full):
                    made[2 * pair, a * full + t] = tile(a, t)
                    made[2 * pair + 1, a * full + t] = tile(a, full + 1 + t)
            first = tile(0, full).astype(jnp.float32)
            second = pltpu.roll(tile(1, full).astype(jnp.float32), half, 1)
            third = tile(2, full)
            made[2 * pair, 3 * full] = jnp.where(lane < half, first, second).astype(jnp.bfloat16)
            made[2 * pair + 1, 3 * full] = jnp.where(lane < half, second, first).astype(jnp.bfloat16)
            made[2 * pair, 3 * full + 1] = third
            made[2 * pair + 1, 3 * full + 1] = third

    def moved(field, i, owner):
        _, made, got = fields[field]
        peer = lax.rem(me + i, n)
        return pltpu.make_async_remote_copy(
            src_ref=made.at[peer],
            dst_ref=got.at[owner],
            send_sem=send_sem.at[field, i],
            recv_sem=recv_sem.at[field, i],
            device_id={"cx": peer},
        )

    raw_copies[0].wait()
    pack(0)
    pl.semaphore_wait(barrier, n - 1)

    @pl.loop(1, n)
    def _(i):
        moved(0, i, me).start()

    own_copies[0].start()
    for copy in phi_copies:
        copy.start()
    raw_copies[1].wait()
    pack(1)
    own_copies[1].start()

    for copy in small_copies:
        copy.wait()
    width = pick.shape[2]
    odd = lax.rem(me, 2)
    at = lax.broadcasted_iota(jnp.int32, (size, width), 1).astype(jnp.float32)
    for c in range(layer):
        local = atoms[c : c + 1, :] - me * span
        moved_on = jnp.where(local < half, local + (edge + half), local - half)
        place = jnp.where(odd == 1, moved_on, local)
        other = jnp.where(
            place >= edge, jnp.where(place >= edge + half, place - half, place + half), place
        )
        for i, row in enumerate((place, other)):
            pick[i, c * size : (c + 1) * size, :] = jnp.where(
                at == column(row.astype(jnp.float32)), 1.0, 0.0
            ).astype(jnp.bfloat16)
    configs = order.shape[1]
    match = order[...] == lax.broadcasted_iota(jnp.int32, (configs, configs), 0)
    wt[...] = jnp.sum(jnp.where(match, column(weights[...]), 0.0), axis=0, keepdims=True)

    @pl.loop(1, n)
    def _(i):
        moved(0, i, me).wait_send()
        moved(1, i, me).start()

    def gathered(field, store):
        own_copies[field].wait()

        @pl.loop(1, n)
        def _(i):
            moved(field, i, lax.rem(me + n - i, n)).wait_recv()

        for a in range(3):
            got = fields[field][2]
            tiles = [a * full + t for t in range(full)] + [3 * full + a // 2]
            x = jnp.concatenate([got[:, t].reshape(n * padded, LANES) for t in tiles], axis=1)
            y = lax.dot_general(pick[a % 2], x, NT, preferred_element_type=jnp.float32)
            if padded != rows:
                sub = lax.broadcasted_iota(jnp.int32, (n * padded, n * rows), 0)
                col = lax.broadcasted_iota(jnp.int32, (n * padded, n * rows), 1)
                keep = sub == col // rows * padded + col % rows
                y = jnp.dot(
                    y.astype(jnp.bfloat16),
                    jnp.where(keep, 1.0, 0.0).astype(jnp.bfloat16),
                    preferred_element_type=jnp.float32,
                )
            for c in range(layer):
                store(c, a, y[c * size : (c + 1) * size, :])

    def keep_disp(c, a, value):
        cdisp[layer + c, a * size : (a + 1) * size, :] = value.astype(jnp.bfloat16)

    def keep_force(c, a, value):
        cforce[c, a * size : (a + 1) * size, :] = value

    gathered(0, keep_disp)
    middle = pl.ds(layer, layer)
    halo = [
        pltpu.make_async_remote_copy(
            src_ref=cdisp.at[middle],
            dst_ref=cdisp.at[pl.ds(place, layer)],
            send_sem=halo_send.at[i],
            recv_sem=halo_recv.at[i],
            device_id={"cx": peer},
        )
        for i, (peer, place) in enumerate(((right, 0), (left, 2 * layer)))
    ]
    for copy in halo:
        copy.start()
    gathered(1, keep_force)
    for copy in halo:
        copy.wait_recv()
    disp_out = pltpu.make_async_copy(cdisp, frame_disp, out_sem.at[0])
    disp_out.start()
    for copy in phi_copies:
        copy.wait()

    def back(c, side):
        peer, place = ((right, 0), (left, 2 * layer))[side]
        return pltpu.make_async_remote_copy(
            src_ref=resid.at[c],
            dst_ref=frame_resid.at[place + c],
            send_sem=back_send.at[side, c],
            recv_sem=back_recv.at[side, c],
            device_id={"cx": peer},
        )

    def keep(c):
        return pltpu.make_async_copy(resid.at[c], frame_resid.at[layer + c], out_sem.at[1 + c])

    dof = 3 * size

    @pl.loop(0, layer)
    def _(c):
        total = cforce[c]
        for k in range(blocks):
            name = near[c, k]
            offset = jnp.minimum(lax.rem(name // layer - me + 1 + n, n), 2)
            total += jnp.dot(
                phi_v[c, k],
                cdisp[offset * layer + lax.rem(name, layer)],
                preferred_element_type=jnp.float32,
            )
        rounded = total.astype(jnp.bfloat16)
        resid[c] = rounded
        back(c, 0).start()
        back(c, 1).start()
        keep(c).start()
        sides[c, :, :configs] = (rounded.astype(jnp.float32) * wt[...]).astype(jnp.bfloat16)
        sides[c, :, configs:] = (cdisp[layer + c].astype(jnp.float32) * wt[...]).astype(
            jnp.bfloat16
        )

    @pl.loop(1, n)
    def _(i):
        moved(1, i, me).wait_send()

    for copy in halo:
        copy.wait_send()
    disp_out.wait()
    for c in range(layer):
        keep(c).wait()
        for side in range(2):
            back(c, side).wait()


def products(n, layer, near, position, sides, disp, resid, residual, gradient):
    c = pl.program_id(0)
    blocks = gradient.shape[1]
    configs = disp.shape[2]
    me = position[0]
    residual[0] = resid[layer + c]
    for k in range(blocks):
        name = near[c, k]
        offset = jnp.minimum(lax.rem(name // layer - me + 1 + n, n), 2)
        index = offset * layer + lax.rem(name, layer)
        total = lax.dot_general(
            sides[0, :, :configs], disp[index], NT, preferred_element_type=jnp.float32
        ) + lax.dot_general(
            sides[0, :, configs:], resid[index], NT, preferred_element_type=jnp.float32
        )
        gradient[0, k] = (0.5 * total).astype(jnp.bfloat16)


def shards(n, displacements, forces, phi, neighbours, cluster_atoms, config_order, weights):
    rows, _, atoms = displacements.shape
    layer, size = cluster_atoms.shape
    blocks, dof = phi.shape[1:3]
    configs = config_order.shape[0]
    span = atoms // n
    full, rest = divmod(span, LANES)
    assert 2 * rest == LANES and n % 2 == 0
    slots, width = 3 * full + 2, (full + 1) * LANES
    padded = -(-rows // SUBLANES) * SUBLANES

    def laid(field):
        field = jnp.transpose(field, (1, 0, 2))
        if padded != rows:
            field = jnp.pad(field, ((0, 0), (0, padded - rows), (0, 0)))
        return field

    bf16 = jnp.bfloat16
    dma = pltpu.SemaphoreType.DMA
    frame = jax.ShapeDtypeStruct((3 * layer, dof, configs), bf16)
    frame_disp, frame_resid, sides = pl.pallas_call(
        functools.partial(exchange, n, rows, span),
        out_shape=[frame, frame, jax.ShapeDtypeStruct((layer, dof, 2 * configs), bf16)],
        in_specs=[ANY] * 7,
        out_specs=[ANY, ANY, VMEM],
        scratch_shapes=[
            pltpu.SMEM(neighbours.shape, jnp.int32),
            pltpu.VMEM(cluster_atoms.shape, jnp.int32),
            pltpu.VMEM((1, configs), jnp.int32),
            pltpu.VMEM((1, configs), jnp.float32),
            pltpu.VMEM(phi.shape, bf16),
            *[pltpu.VMEM((3, padded, atoms), bf16)] * 2,
            *[pltpu.VMEM((n, slots, padded, LANES), bf16)] * 4,
            pltpu.VMEM((2, layer * size, width), bf16),
            pltpu.VMEM((3 * layer, dof, configs), bf16),
            pltpu.VMEM((layer, dof, configs), jnp.float32),
            pltpu.VMEM((layer, dof, configs), bf16),
            pltpu.VMEM((1, configs), jnp.float32),
            dma((4,)),
            dma((2,)),
            dma((2,)),
            dma((layer,)),
            dma((2, n)),
            dma((2, n)),
            dma((2,)),
            dma((2,)),
            dma((2, layer)),
            dma((2, layer)),
            dma((1 + layer,)),
        ],
        compiler_params=pltpu.CompilerParams(
            collective_id=0, has_side_effects=True, vmem_limit_bytes=60 * 1024 * 1024
        ),
    )(
        laid(displacements),
        laid(forces),
        phi,
        neighbours,
        cluster_atoms,
        config_order.reshape(1, configs),
        weights.reshape(1, configs),
    )
    position = lax.axis_index("cx").reshape(1).astype(jnp.int32)
    whole = pl.BlockSpec((3 * layer, dof, configs), lambda c: (0, 0, 0))
    return pl.pallas_call(
        functools.partial(products, n, layer),
        grid=(layer,),
        out_shape=[
            jax.ShapeDtypeStruct((layer, dof, configs), bf16),
            jax.ShapeDtypeStruct(phi.shape, bf16),
        ],
        in_specs=[
            SMEM,
            SMEM,
            pl.BlockSpec((1, dof, 2 * configs), lambda c: (c, 0, 0)),
            whole,
            whole,
        ],
        out_specs=[
            pl.BlockSpec((1, dof, configs), lambda c: (c, 0, 0)),
            pl.BlockSpec((1, blocks, dof, dof), lambda c: (c, 0, 0, 0)),
        ],
        compiler_params=pltpu.CompilerParams(vmem_limit_bytes=60 * 1024 * 1024),
    )(neighbours, position, sides, frame_disp, frame_resid)


def solution(mesh):
    in_specs = (
        P(("groups", "cx"), None, None),
        P(("groups", "cx"), None, None),
        P(("groups", "cx"), None, None, None),
        P("cx", None),
        P("cx", None),
        P("groups"),
        P("groups"),
    )
    out_specs = (P(("groups", "cx"), None, None), P(("groups", "cx"), None, None, None))
    return jax.shard_map(
        functools.partial(shards, mesh.shape["cx"]),
        mesh=mesh,
        in_specs=in_specs,
        out_specs=out_specs,
        check_vma=False,
    )
```

```python
import functools

import jax
import jax.numpy as jnp
from jax import lax
from jax.experimental import pallas as pl
from jax.experimental.pallas import tpu as pltpu
from jax.sharding import PartitionSpec as P

LANES = 128
SUBLANES = 16
ANY = pl.BlockSpec(memory_space=pl.ANY)
VMEM = pl.BlockSpec(memory_space=pltpu.VMEM)
SMEM = pl.BlockSpec(memory_space=pltpu.SMEM)
NT = (((1,), (1,)), ((), ()))


def column(row):
    m = row.shape[1]
    eye = lax.broadcasted_iota(jnp.int32, (m, m), 0) == lax.broadcasted_iota(
        jnp.int32, (m, m), 1
    )
    return jnp.sum(jnp.where(eye, row, jnp.zeros_like(row)), axis=1, keepdims=True)


def exchange(
    n, rows, span,
    disp, force, phi, near_in, atoms_in, order_in, weights_in,
    frame_resid, sides, part_out,
    near, atoms, order, weights,
    phi_v, part, raw_disp, raw_force, made_disp, made_force, got_disp, got_force, pick, cdisp, cforce, resid, wt, small_sem,
    raw_sem, own_sem, phi_sem, send_sem, recv_sem, halo_send, halo_recv, back_send, back_recv, out_sem, part_sem,
):
    layer, size = atoms.shape
    blocks = phi.shape[1]
    slots, padded = got_disp.shape[1:3]
    full = (slots - 2) // 3
    edge = full * LANES
    half = LANES // 2
    me = lax.axis_index("cx")
    right, left = lax.rem(me + 1, n), lax.rem(me + n - 1, n)

    phi_copies = [
        pltpu.make_async_copy(phi.at[c], phi_v.at[c], phi_sem.at[c]) for c in range(layer)
    ]
    fields = ((raw_disp, made_disp, got_disp), (raw_force, made_force, got_force))
    raw_copies = [
        pltpu.make_async_copy(src, fields[i][0], raw_sem.at[i]) for i, src in enumerate((disp, force))
    ]
    own_copies = [
        pltpu.make_async_copy(made.at[me], got.at[me], own_sem.at[i])
        for i, (_, made, got) in enumerate(fields)
    ]
    small_copies = [
        pltpu.make_async_copy(src, dst, small_sem.at[i])
        for i, (src, dst) in enumerate(
            ((near_in, near), (atoms_in, atoms), (order_in, order), (weights_in, weights))
        )
    ]
    barrier = pltpu.get_barrier_semaphore()

    @pl.loop(1, n)
    def _(i):
        pl.semaphore_signal(barrier, inc=1, device_id={"cx": lax.rem(me + i, n)})

    for copy in raw_copies + small_copies:
        copy.start()

    lane = lax.broadcasted_iota(jnp.int32, (padded, LANES), 1)

    def pack(field):
        raw, made, _ = fields[field]

        @pl.loop(0, n // 2)
        def _(pair):
            base = pair * (2 * span)

            def tile(a, t):
                return raw[a, :, pl.ds(pl.multiple_of(base + t * LANES, LANES), LANES)]

            for a in range(3):
                for t in range(full):
                    made[2 * pair, a * full + t] = tile(a, t)
                    made[2 * pair + 1, a * full + t] = tile(a, full + 1 + t)
            first = tile(0, full).astype(jnp.float32)
            second = pltpu.roll(tile(1, full).astype(jnp.float32), half, 1)
            third = tile(2, full)
            made[2 * pair, 3 * full] = jnp.where(lane < half, first, second).astype(jnp.bfloat16)
            made[2 * pair + 1, 3 * full] = jnp.where(lane < half, second, first).astype(jnp.bfloat16)
            made[2 * pair, 3 * full + 1] = third
            made[2 * pair + 1, 3 * full + 1] = third

    def moved(field, i, owner):
        _, made, got = fields[field]
        peer = lax.rem(me + i, n)
        return pltpu.make_async_remote_copy(
            src_ref=made.at[peer],
            dst_ref=got.at[owner],
            send_sem=send_sem.at[field, i],
            recv_sem=recv_sem.at[field, i],
            device_id={"cx": peer},
        )

    raw_copies[0].wait()
    pack(0)
    pl.semaphore_wait(barrier, n - 1)

    @pl.loop(1, n)
    def _(i):
        moved(0, i, me).start()

    own_copies[0].start()
    for copy in phi_copies:
        copy.start()
    raw_copies[1].wait()
    pack(1)
    own_copies[1].start()

    for copy in small_copies:
        copy.wait()
    width = pick.shape[2]
    odd = lax.rem(me, 2)
    at = lax.broadcasted_iota(jnp.int32, (size, width), 1).astype(jnp.float32)
    for c in range(layer):
        local = atoms[c : c + 1, :] - me * span
        moved_on = jnp.where(local < half, local + (edge + half), local - half)
        place = jnp.where(odd == 1, moved_on, local)
        other = jnp.where(
            place >= edge, jnp.where(place >= edge + half, place - half, place + half), place
        )
        for i, row in enumerate((place, other)):
            pick[i, c * size : (c + 1) * size, :] = jnp.where(
                at == column(row.astype(jnp.float32)), 1.0, 0.0
            ).astype(jnp.bfloat16)
    configs = order.shape[1]
    match = order[...] == lax.broadcasted_iota(jnp.int32, (configs, configs), 0)
    wt[...] = jnp.sum(jnp.where(match, column(weights[...]), 0.0), axis=0, keepdims=True)

    @pl.loop(1, n)
    def _(i):
        moved(0, i, me).wait_send()
        moved(1, i, me).start()

    def gathered(field, store):
        own_copies[field].wait()

        @pl.loop(1, n)
        def _(i):
            moved(field, i, lax.rem(me + n - i, n)).wait_recv()

        for a in range(3):
            got = fields[field][2]
            tiles = [a * full + t for t in range(full)] + [3 * full + a // 2]
            x = jnp.concatenate([got[:, t].reshape(n * padded, LANES) for t in tiles], axis=1)
            y = lax.dot_general(pick[a % 2], x, NT, preferred_element_type=jnp.float32)
            if padded != rows:
                sub = lax.broadcasted_iota(jnp.int32, (n * padded, n * rows), 0)
                col = lax.broadcasted_iota(jnp.int32, (n * padded, n * rows), 1)
                keep = sub == col // rows * padded + col % rows
                y = jnp.dot(
                    y.astype(jnp.bfloat16),
                    jnp.where(keep, 1.0, 0.0).astype(jnp.bfloat16),
                    preferred_element_type=jnp.float32,
                )
            for c in range(layer):
                store(c, a, y[c * size : (c + 1) * size, :])

    def keep_disp(c, a, value):
        cdisp[layer + c, a * size : (a + 1) * size, :] = value.astype(jnp.bfloat16)

    def keep_force(c, a, value):
        cforce[c, a * size : (a + 1) * size, :] = value

    gathered(0, keep_disp)
    middle = pl.ds(layer, layer)
    halo = [
        pltpu.make_async_remote_copy(
            src_ref=cdisp.at[middle],
            dst_ref=cdisp.at[pl.ds(place, layer)],
            send_sem=halo_send.at[i],
            recv_sem=halo_recv.at[i],
            device_id={"cx": peer},
        )
        for i, (peer, place) in enumerate(((right, 0), (left, 2 * layer)))
    ]
    for copy in halo:
        copy.start()
    gathered(1, keep_force)
    for copy in halo:
        copy.wait_recv()
    for copy in phi_copies:
        copy.wait()

    def back(c, side):
        peer, place = ((right, 0), (left, 2 * layer))[side]
        return pltpu.make_async_remote_copy(
            src_ref=resid.at[c],
            dst_ref=frame_resid.at[place + c],
            send_sem=back_send.at[side, c],
            recv_sem=back_recv.at[side, c],
            device_id={"cx": peer},
        )

    def keep(c):
        return pltpu.make_async_copy(resid.at[c], frame_resid.at[layer + c], out_sem.at[c])

    def beside(c, k):
        name = near[c, k]
        offset = jnp.minimum(lax.rem(name // layer - me + 1 + n, n), 2)
        return cdisp[offset * layer + lax.rem(name, layer)]

    @pl.loop(0, layer)
    def _(c):
        total = cforce[c]
        for k in range(blocks):
            total += jnp.dot(phi_v[c, k], beside(c, k), preferred_element_type=jnp.float32)
        rounded = total.astype(jnp.bfloat16)
        resid[c] = rounded
        back(c, 0).start()
        back(c, 1).start()
        keep(c).start()

    def part_copy(c):
        return pltpu.make_async_copy(part.at[c], part_out.at[c], part_sem.at[c])

    @pl.loop(0, layer)
    def _(c):
        wres = (resid[c].astype(jnp.float32) * wt[...]).astype(jnp.bfloat16)
        sides[c] = (cdisp[layer + c].astype(jnp.float32) * wt[...]).astype(jnp.bfloat16)
        for k in range(blocks):
            part[c, k] = lax.dot_general(
                wres, beside(c, k), NT, preferred_element_type=jnp.float32
            ).astype(jnp.bfloat16)
        part_copy(c).start()

    @pl.loop(1, n)
    def _(i):
        moved(1, i, me).wait_send()

    for copy in halo:
        copy.wait_send()
    for c in range(layer):
        keep(c).wait()
        part_copy(c).wait()
        for side in range(2):
            back(c, side).wait()


def products(n, layer, near, position, sides, part, resid, residual, gradient):
    c = pl.program_id(0)
    blocks = gradient.shape[1]
    me = position[0]
    residual[0] = resid[layer + c]
    for k in range(blocks):
        name = near[c, k]
        offset = jnp.minimum(lax.rem(name // layer - me + 1 + n, n), 2)
        index = offset * layer + lax.rem(name, layer)
        total = part[0, k].astype(jnp.float32) + lax.dot_general(
            sides[0], resid[index], NT, preferred_element_type=jnp.float32
        )
        gradient[0, k] = (0.5 * total).astype(jnp.bfloat16)


def shards(n, displacements, forces, phi, neighbours, cluster_atoms, config_order, weights):
    rows, _, atoms = displacements.shape
    layer, size = cluster_atoms.shape
    blocks, dof = phi.shape[1:3]
    configs = config_order.shape[0]
    span = atoms // n
    full, rest = divmod(span, LANES)
    assert 2 * rest == LANES and n % 2 == 0
    slots, width = 3 * full + 2, (full + 1) * LANES
    padded = -(-rows // SUBLANES) * SUBLANES

    def laid(field):
        field = jnp.transpose(field, (1, 0, 2))
        if padded != rows:
            field = jnp.pad(field, ((0, 0), (0, padded - rows), (0, 0)))
        return field

    bf16 = jnp.bfloat16
    dma = pltpu.SemaphoreType.DMA
    frame = jax.ShapeDtypeStruct((3 * layer, dof, configs), bf16)
    frame_resid, sides, part = pl.pallas_call(
        functools.partial(exchange, n, rows, span),
        out_shape=[
            frame,
            jax.ShapeDtypeStruct((layer, dof, configs), bf16),
            jax.ShapeDtypeStruct(phi.shape, bf16),
        ],
        in_specs=[ANY] * 7,
        out_specs=[ANY, VMEM, ANY],
        scratch_shapes=[
            pltpu.SMEM(neighbours.shape, jnp.int32),
            pltpu.VMEM(cluster_atoms.shape, jnp.int32),
            pltpu.VMEM((1, configs), jnp.int32),
            pltpu.VMEM((1, configs), jnp.float32),
            *[pltpu.VMEM(phi.shape, bf16)] * 2,
            *[pltpu.VMEM((3, padded, atoms), bf16)] * 2,
            *[pltpu.VMEM((n, slots, padded, LANES), bf16)] * 4,
            pltpu.VMEM((2, layer * size, width), bf16),
            pltpu.VMEM((3 * layer, dof, configs), bf16),
            pltpu.VMEM((layer, dof, configs), jnp.float32),
            pltpu.VMEM((layer, dof, configs), bf16),
            pltpu.VMEM((1, configs), jnp.float32),
            dma((4,)),
            dma((2,)),
            dma((2,)),
            dma((layer,)),
            dma((2, n)),
            dma((2, n)),
            dma((2,)),
            dma((2,)),
            dma((2, layer)),
            dma((2, layer)),
            dma((layer,)),
            dma((layer,)),
        ],
        compiler_params=pltpu.CompilerParams(
            collective_id=0, has_side_effects=True, vmem_limit_bytes=60 * 1024 * 1024
        ),
    )(
        laid(displacements),
        laid(forces),
        phi,
        neighbours,
        cluster_atoms,
        config_order.reshape(1, configs),
        weights.reshape(1, configs),
    )
    position = lax.axis_index("cx").reshape(1).astype(jnp.int32)
    return pl.pallas_call(
        functools.partial(products, n, layer),
        grid=(layer,),
        out_shape=[
            jax.ShapeDtypeStruct((layer, dof, configs), bf16),
            jax.ShapeDtypeStruct(phi.shape, bf16),
        ],
        in_specs=[
            SMEM,
            SMEM,
            pl.BlockSpec((1, dof, configs), lambda c: (c, 0, 0)),
            pl.BlockSpec((1, blocks, dof, dof), lambda c: (c, 0, 0, 0)),
            pl.BlockSpec((3 * layer, dof, configs), lambda c: (0, 0, 0)),
        ],
        out_specs=[
            pl.BlockSpec((1, dof, configs), lambda c: (c, 0, 0)),
            pl.BlockSpec((1, blocks, dof, dof), lambda c: (c, 0, 0, 0)),
        ],
        compiler_params=pltpu.CompilerParams(vmem_limit_bytes=60 * 1024 * 1024),
    )(neighbours, position, sides, part, frame_resid)


def solution(mesh):
    in_specs = (
        P(("groups", "cx"), None, None),
        P(("groups", "cx"), None, None),
        P(("groups", "cx"), None, None, None),
        P("cx", None),
        P("cx", None),
        P("groups"),
        P("groups"),
    )
    out_specs = (P(("groups", "cx"), None, None), P(("groups", "cx"), None, None, None))
    return jax.shard_map(
        functools.partial(shards, mesh.shape["cx"]),
        mesh=mesh,
        in_specs=in_specs,
        out_specs=out_specs,
        check_vma=False,
    )
```

```python
import functools

import jax
import jax.numpy as jnp
from jax import lax
from jax.experimental import pallas as pl
from jax.experimental.pallas import tpu as pltpu
from jax.sharding import PartitionSpec as P

LANES = 128
SUBLANES = 16
ANY = pl.BlockSpec(memory_space=pl.ANY)
VMEM = pl.BlockSpec(memory_space=pltpu.VMEM)
SMEM = pl.BlockSpec(memory_space=pltpu.SMEM)
NT = (((1,), (1,)), ((), ()))


def column(row):
    m = row.shape[1]
    eye = lax.broadcasted_iota(jnp.int32, (m, m), 0) == lax.broadcasted_iota(
        jnp.int32, (m, m), 1
    )
    return jnp.sum(jnp.where(eye, row, jnp.zeros_like(row)), axis=1, keepdims=True)


def exchange(
    n, rows, span,
    disp, force, phi, near_in, atoms_in, order_in, weights_in,
    frame_disp, frame_resid, sides,
    near, atoms, order, weights,
    phi_v, raw_disp, raw_force, made_disp, made_force, got_disp, got_force, pick, cdisp, cforce, resid, wt, small_sem,
    raw_sem, own_sem, phi_sem, send_sem, recv_sem, halo_send, halo_recv, back_send, back_recv, out_sem,
):
    layer, size = atoms.shape
    blocks = phi.shape[1]
    slots, padded = got_disp.shape[1:3]
    full = (slots - 2) // 3
    edge = full * LANES
    half = LANES // 2
    me = lax.axis_index("cx")
    right, left = lax.rem(me + 1, n), lax.rem(me + n - 1, n)

    phi_copies = [
        pltpu.make_async_copy(phi.at[c], phi_v.at[c], phi_sem.at[c]) for c in range(layer)
    ]
    fields = ((raw_disp, made_disp, got_disp), (raw_force, made_force, got_force))
    raw_copies = [
        pltpu.make_async_copy(src, fields[i][0], raw_sem.at[i]) for i, src in enumerate((disp, force))
    ]
    own_copies = [
        pltpu.make_async_copy(made.at[me], got.at[me], own_sem.at[i])
        for i, (_, made, got) in enumerate(fields)
    ]
    small_copies = [
        pltpu.make_async_copy(src, dst, small_sem.at[i])
        for i, (src, dst) in enumerate(
            ((near_in, near), (atoms_in, atoms), (order_in, order), (weights_in, weights))
        )
    ]
    barrier = pltpu.get_barrier_semaphore()

    @pl.loop(1, n)
    def _(i):
        pl.semaphore_signal(barrier, inc=1, device_id={"cx": lax.rem(me + i, n)})

    for copy in raw_copies + small_copies:
        copy.start()

    lane = lax.broadcasted_iota(jnp.int32, (padded, LANES), 1)

    def pack(field):
        raw, made, _ = fields[field]

        @pl.loop(0, n // 2)
        def _(pair):
            base = pair * (2 * span)

            def tile(a, t):
                return raw[a, :, pl.ds(pl.multiple_of(base + t * LANES, LANES), LANES)]

            for a in range(3):
                for t in range(full):
                    made[2 * pair, a * full + t] = tile(a, t)
                    made[2 * pair + 1, a * full + t] = tile(a, full + 1 + t)
            first = tile(0, full).astype(jnp.float32)
            second = pltpu.roll(tile(1, full).astype(jnp.float32), half, 1)
            third = tile(2, full)
            made[2 * pair, 3 * full] = jnp.where(lane < half, first, second).astype(jnp.bfloat16)
            made[2 * pair + 1, 3 * full] = jnp.where(lane < half, second, first).astype(jnp.bfloat16)
            made[2 * pair, 3 * full + 1] = third
            made[2 * pair + 1, 3 * full + 1] = third

    def moved(field, i, owner):
        _, made, got = fields[field]
        peer = lax.rem(me + i, n)
        return pltpu.make_async_remote_copy(
            src_ref=made.at[peer],
            dst_ref=got.at[owner],
            send_sem=send_sem.at[field, i],
            recv_sem=recv_sem.at[field, i],
            device_id={"cx": peer},
        )

    raw_copies[0].wait()
    pack(0)
    pl.semaphore_wait(barrier, n - 1)

    @pl.loop(1, n)
    def _(i):
        moved(0, i, me).start()

    own_copies[0].start()
    for copy in phi_copies:
        copy.start()
    raw_copies[1].wait()
    pack(1)
    own_copies[1].start()

    for copy in small_copies:
        copy.wait()
    width = pick.shape[2]
    odd = lax.rem(me, 2)
    at = lax.broadcasted_iota(jnp.int32, (size, width), 1).astype(jnp.float32)
    for c in range(layer):
        local = atoms[c : c + 1, :] - me * span
        moved_on = jnp.where(local < half, local + (edge + half), local - half)
        place = jnp.where(odd == 1, moved_on, local)
        other = jnp.where(
            place >= edge, jnp.where(place >= edge + half, place - half, place + half), place
        )
        for i, row in enumerate((place, other)):
            pick[i, c * size : (c + 1) * size, :] = jnp.where(
                at == column(row.astype(jnp.float32)), 1.0, 0.0
            ).astype(jnp.bfloat16)
    configs = order.shape[1]
    match = order[...] == lax.broadcasted_iota(jnp.int32, (configs, configs), 0)
    wt[...] = jnp.sum(jnp.where(match, column(weights[...]), 0.0), axis=0, keepdims=True)

    @pl.loop(1, n // 2)
    def _(i):
        moved(0, i, me).wait_send()
        moved(1, i, me).start()

    def gathered(field, store):
        own_copies[field].wait()

        @pl.loop(1, n)
        def _(i):
            moved(field, i, lax.rem(me + n - i, n)).wait_recv()

        for a in range(3):
            got = fields[field][2]
            tiles = [a * full + t for t in range(full)] + [3 * full + a // 2]
            x = jnp.concatenate([got[:, t].reshape(n * padded, LANES) for t in tiles], axis=1)
            y = lax.dot_general(pick[a % 2], x, NT, preferred_element_type=jnp.float32)
            if padded != rows:
                sub = lax.broadcasted_iota(jnp.int32, (n * padded, n * rows), 0)
                col = lax.broadcasted_iota(jnp.int32, (n * padded, n * rows), 1)
                keep = sub == col // rows * padded + col % rows
                y = jnp.dot(
                    y.astype(jnp.bfloat16),
                    jnp.where(keep, 1.0, 0.0).astype(jnp.bfloat16),
                    preferred_element_type=jnp.float32,
                )
            for c in range(layer):
                store(c, a, y[c * size : (c + 1) * size, :])

    def keep_disp(c, a, value):
        cdisp[layer + c, a * size : (a + 1) * size, :] = value.astype(jnp.bfloat16)

    def keep_force(c, a, value):
        cforce[c, a * size : (a + 1) * size, :] = value

    gathered(0, keep_disp)
    middle = pl.ds(layer, layer)
    halo = [
        pltpu.make_async_remote_copy(
            src_ref=cdisp.at[middle],
            dst_ref=cdisp.at[pl.ds(place, layer)],
            send_sem=halo_send.at[i],
            recv_sem=halo_recv.at[i],
            device_id={"cx": peer},
        )
        for i, (peer, place) in enumerate(((right, 0), (left, 2 * layer)))
    ]
    for copy in halo:
        copy.start()

    @pl.loop(n // 2, n)
    def _(i):
        moved(0, i, me).wait_send()
        moved(1, i, me).start()

    gathered(1, keep_force)
    for copy in halo:
        copy.wait_recv()
    disp_out = pltpu.make_async_copy(cdisp, frame_disp, out_sem.at[0])
    disp_out.start()
    for copy in phi_copies:
        copy.wait()

    def back(c, side):
        peer, place = ((right, 0), (left, 2 * layer))[side]
        return pltpu.make_async_remote_copy(
            src_ref=resid.at[c],
            dst_ref=frame_resid.at[place + c],
            send_sem=back_send.at[side, c],
            recv_sem=back_recv.at[side, c],
            device_id={"cx": peer},
        )

    def keep(c):
        return pltpu.make_async_copy(resid.at[c], frame_resid.at[layer + c], out_sem.at[1 + c])

    dof = 3 * size

    @pl.loop(0, layer)
    def _(c):
        total = cforce[c]
        for k in range(blocks):
            name = near[c, k]
            offset = jnp.minimum(lax.rem(name // layer - me + 1 + n, n), 2)
            total += jnp.dot(
                phi_v[c, k],
                cdisp[offset * layer + lax.rem(name, layer)],
                preferred_element_type=jnp.float32,
            )
        rounded = total.astype(jnp.bfloat16)
        resid[c] = rounded
        back(c, 0).start()
        back(c, 1).start()
        keep(c).start()
        sides[c, :, :configs] = (rounded.astype(jnp.float32) * wt[...]).astype(jnp.bfloat16)
        sides[c, :, configs:] = (cdisp[layer + c].astype(jnp.float32) * wt[...]).astype(
            jnp.bfloat16
        )

    @pl.loop(1, n)
    def _(i):
        moved(1, i, me).wait_send()

    for copy in halo:
        copy.wait_send()
    disp_out.wait()
    for c in range(layer):
        keep(c).wait()
        for side in range(2):
            back(c, side).wait()


def products(n, layer, near, position, sides, disp, resid, residual, gradient):
    c = pl.program_id(0)
    blocks = gradient.shape[1]
    configs = disp.shape[2]
    me = position[0]
    residual[0] = resid[layer + c]
    for k in range(blocks):
        name = near[c, k]
        offset = jnp.minimum(lax.rem(name // layer - me + 1 + n, n), 2)
        index = offset * layer + lax.rem(name, layer)
        total = lax.dot_general(
            sides[0, :, :configs], disp[index], NT, preferred_element_type=jnp.float32
        ) + lax.dot_general(
            sides[0, :, configs:], resid[index], NT, preferred_element_type=jnp.float32
        )
        gradient[0, k] = (0.5 * total).astype(jnp.bfloat16)


def shards(n, displacements, forces, phi, neighbours, cluster_atoms, config_order, weights):
    rows, _, atoms = displacements.shape
    layer, size = cluster_atoms.shape
    blocks, dof = phi.shape[1:3]
    configs = config_order.shape[0]
    span = atoms // n
    full, rest = divmod(span, LANES)
    assert 2 * rest == LANES and n % 2 == 0
    slots, width = 3 * full + 2, (full + 1) * LANES
    padded = -(-rows // SUBLANES) * SUBLANES

    def laid(field):
        field = jnp.transpose(field, (1, 0, 2))
        if padded != rows:
            field = jnp.pad(field, ((0, 0), (0, padded - rows), (0, 0)))
        return field

    bf16 = jnp.bfloat16
    dma = pltpu.SemaphoreType.DMA
    frame = jax.ShapeDtypeStruct((3 * layer, dof, configs), bf16)
    frame_disp, frame_resid, sides = pl.pallas_call(
        functools.partial(exchange, n, rows, span),
        out_shape=[frame, frame, jax.ShapeDtypeStruct((layer, dof, 2 * configs), bf16)],
        in_specs=[ANY] * 7,
        out_specs=[ANY, ANY, VMEM],
        scratch_shapes=[
            pltpu.SMEM(neighbours.shape, jnp.int32),
            pltpu.VMEM(cluster_atoms.shape, jnp.int32),
            pltpu.VMEM((1, configs), jnp.int32),
            pltpu.VMEM((1, configs), jnp.float32),
            pltpu.VMEM(phi.shape, bf16),
            *[pltpu.VMEM((3, padded, atoms), bf16)] * 2,
            *[pltpu.VMEM((n, slots, padded, LANES), bf16)] * 4,
            pltpu.VMEM((2, layer * size, width), bf16),
            pltpu.VMEM((3 * layer, dof, configs), bf16),
            pltpu.VMEM((layer, dof, configs), jnp.float32),
            pltpu.VMEM((layer, dof, configs), bf16),
            pltpu.VMEM((1, configs), jnp.float32),
            dma((4,)),
            dma((2,)),
            dma((2,)),
            dma((layer,)),
            dma((2, n)),
            dma((2, n)),
            dma((2,)),
            dma((2,)),
            dma((2, layer)),
            dma((2, layer)),
            dma((1 + layer,)),
        ],
        compiler_params=pltpu.CompilerParams(
            collective_id=0, has_side_effects=True, vmem_limit_bytes=60 * 1024 * 1024
        ),
    )(
        laid(displacements),
        laid(forces),
        phi,
        neighbours,
        cluster_atoms,
        config_order.reshape(1, configs),
        weights.reshape(1, configs),
    )
    position = lax.axis_index("cx").reshape(1).astype(jnp.int32)
    whole = pl.BlockSpec((3 * layer, dof, configs), lambda c: (0, 0, 0))
    return pl.pallas_call(
        functools.partial(products, n, layer),
        grid=(layer,),
        out_shape=[
            jax.ShapeDtypeStruct((layer, dof, configs), bf16),
            jax.ShapeDtypeStruct(phi.shape, bf16),
        ],
        in_specs=[
            SMEM,
            SMEM,
            pl.BlockSpec((1, dof, 2 * configs), lambda c: (c, 0, 0)),
            whole,
            whole,
        ],
        out_specs=[
            pl.BlockSpec((1, dof, configs), lambda c: (c, 0, 0)),
            pl.BlockSpec((1, blocks, dof, dof), lambda c: (c, 0, 0, 0)),
        ],
        compiler_params=pltpu.CompilerParams(vmem_limit_bytes=60 * 1024 * 1024),
    )(neighbours, position, sides, frame_disp, frame_resid)


def solution(mesh):
    in_specs = (
        P(("groups", "cx"), None, None),
        P(("groups", "cx"), None, None),
        P(("groups", "cx"), None, None, None),
        P("cx", None),
        P("cx", None),
        P("groups"),
        P("groups"),
    )
    out_specs = (P(("groups", "cx"), None, None), P(("groups", "cx"), None, None, None))
    return jax.shard_map(
        functools.partial(shards, mesh.shape["cx"]),
        mesh=mesh,
        in_specs=in_specs,
        out_specs=out_specs,
        check_vma=False,
    )
```
